256 devices in a mesh: ctx: 128 (over z, y_hi, x, core), heads: 2 (over y_lo).
Axes of the slice: x: 4, y: 4 (y_hi: 2, y_lo: 2; y = y_hi * 2 + y_lo), z: 8, core: 2. Of those that a mesh axis runs over, the one named last changes fastest.
Arguments:
- queries: bfloat16 [16384, 4096], P('ctx', 'heads'), may hold values from -8 to 8
- key_matrix: bfloat16 [16384, 512], P('ctx', 'heads'), may hold values from -4 to 4
- value_matrix: bfloat16 [16384, 512], P('ctx', 'heads'), may hold values from -6 to 6
- out_weight: bfloat16 [4096, 2560], P('heads'), may hold values from -0.09375 to 0.09375
Outputs:
- projected: bfloat16 [16384, 2560], P(('ctx', 'heads'))
The draws below stay inside these ranges and needn't reach their ends.
All inputs are finite; a program needn't handle non-finite values.
Results may differ from the reference program's by a relative error of at most 0.008.
Values may be sent and summed in bfloat16 or wider, within the bound.
No kernel may reach another device: no remote copies, remote signals or barrier semaphores. Data moves between devices by JAX's collectives and lax.ppermute only.
A program may use at most 128 MiB of HBM per device.

```python
import math
import jax
import jax.numpy as jnp
from jax import lax

QUERY_HEADS = 32
KEY_VALUE_HEADS = 4
HEAD_WIDTH = 128
D = 2560
QUERY_PER_KEY = 8
TOKEN_COUNT = 16384


def sink_signs(key):
    sign_flips = jax.random.bernoulli(jax.random.fold_in(key, 13), 0.5, (KEY_VALUE_HEADS, HEAD_WIDTH))
    return jnp.where(sign_flips, 1.0, -1.0).astype(jnp.float32)


def draw_queries(key, part):
    sink_values = sink_signs(key)
    key = jax.random.fold_in(key, 1)
    sink_rows = 1.5 * jnp.repeat(sink_values, QUERY_HEADS // KEY_VALUE_HEADS, axis=0).reshape(QUERY_HEADS * HEAD_WIDTH)
    base_offset = jnp.clip(3.0 * jax.random.normal(key, (TOKEN_COUNT, QUERY_HEADS * HEAD_WIDTH), jnp.float32) + sink_rows[None, :], -8.0, 8.0)
    return base_offset.astype(jnp.bfloat16)


def draw_key_matrix(key, part):
    sink_values = sink_signs(key)
    key = jax.random.fold_in(key, 2)
    position = jnp.arange(TOKEN_COUNT, dtype=jnp.int32)
    sink_case = position < 3
    sink_rows = 0.74 * sink_values.reshape(KEY_VALUE_HEADS * HEAD_WIDTH)
    base_offset = jnp.clip(jax.random.normal(key, (TOKEN_COUNT, KEY_VALUE_HEADS * HEAD_WIDTH), jnp.float32), -4.0, 4.0)
    base_offset = jnp.where(sink_case[:, None], sink_rows[None, :], base_offset)
    return base_offset.astype(jnp.bfloat16)


def shard_levels(stream_key, shape, split, least, top_value):
    loudness = 1.0
    for dim, shards_of in split:
        draws = jax.random.uniform(jax.random.fold_in(jax.random.fold_in(stream_key, 6), dim), (shards_of,), jnp.float32, least / len(split), top_value / len(split))
        loudness = loudness * jnp.repeat(jnp.exp(draws), shape[dim] // shards_of).reshape((-1,) + (1,) * (len(shape) - 1 - dim))
    return loudness


def noise(key, dims, deviation, reach, shards=(), held_as=jnp.bfloat16):
    loudness = shard_levels(key, dims, shards, -0.22, 0.18) if shards else 1.0
    result = jax.random.normal(key, dims, jnp.float32) * deviation * loudness
    return jnp.minimum(jnp.maximum(result, -reach), reach).astype(held_as)


def setup_inputs(seed: int = 0) -> dict:
    splits = jax.random.split(jax.random.key(seed), 5)
    queries = draw_queries(jax.random.fold_in(splits[4], 71), 0)
    key_matrix = draw_key_matrix(jax.random.fold_in(splits[4], 71), 0)
    value_matrix = noise(splits[2], (TOKEN_COUNT, KEY_VALUE_HEADS * HEAD_WIDTH), 1.0, 6.0, ((0, 128), (1, 2)))
    out_weight = noise(splits[3], (QUERY_HEADS * HEAD_WIDTH, D), (QUERY_HEADS * HEAD_WIDTH) ** -0.5, 0.09375, ((0, 2),))
    return dict(queries=queries, key_matrix=key_matrix, value_matrix=value_matrix, out_weight=out_weight)


far_below_diagonal = -1e+30

def reference(queries, key_matrix, value_matrix, out_weight):
    rows_per_block = math.gcd(TOKEN_COUNT, 1024)
    count_of_blocks = TOKEN_COUNT // rows_per_block
    score_scale = 1.0 / math.sqrt(HEAD_WIDTH)
    query_block_list = queries.reshape(count_of_blocks, rows_per_block, KEY_VALUE_HEADS, QUERY_PER_KEY, HEAD_WIDTH)
    key_block_list = key_matrix.reshape(count_of_blocks, rows_per_block, KEY_VALUE_HEADS, HEAD_WIDTH)
    value_block_list = value_matrix.reshape(count_of_blocks, rows_per_block, KEY_VALUE_HEADS, HEAD_WIDTH)
    inside = jnp.arange(rows_per_block, dtype=jnp.int32)

    def block_scores(query_tile, query_index, key_index):
        key_tile = lax.dynamic_index_in_dim(key_block_list, key_index, 0, keepdims=False)
        scores = jnp.einsum('qgrd,kgd->qgrk', query_tile.astype(jnp.float32), key_tile.astype(jnp.float32)) * score_scale
        query_pos = query_index * rows_per_block + inside
        key_pos = key_index * rows_per_block + inside
        allowed = key_pos[None, :] <= query_pos[:, None]
        return (jnp.where(allowed[:, None, None, :], scores, far_below_diagonal), allowed)

    def one_block(query_index):
        query_tile = lax.dynamic_index_in_dim(query_block_list, query_index, 0, keepdims=False)

        def raise_max(key_index, top_max):
            scores, allowed = block_scores(query_tile, query_index, key_index)
            return jnp.maximum(top_max, lax.optimization_barrier(jnp.max(scores, axis=-1)))
        initial_max = jnp.full((rows_per_block, KEY_VALUE_HEADS, QUERY_PER_KEY), far_below_diagonal, jnp.float32)
        top_max = lax.fori_loop(0, query_index + 1, raise_max, initial_max)

        def accumulate(key_index, carry):
            numerator, weight_sum = carry
            scores, allowed = block_scores(query_tile, query_index, key_index)
            weights = jnp.where(allowed[:, None, None, :], jnp.exp(scores - top_max[..., None]), 0.0)
            weight_sum = weight_sum + lax.optimization_barrier(jnp.sum(weights, axis=-1))
            rounded = lax.optimization_barrier(weights.astype(jnp.bfloat16))
            value_tile = lax.dynamic_index_in_dim(value_block_list, key_index, 0, keepdims=False)
            numerator = numerator + jnp.einsum('qgrk,kgd->qgrd', rounded.astype(jnp.float32), value_tile.astype(jnp.float32))
            return (numerator, weight_sum)
        initial_numerator = jnp.zeros((rows_per_block, KEY_VALUE_HEADS, QUERY_PER_KEY, HEAD_WIDTH), jnp.float32)
        initial_sum = jnp.zeros((rows_per_block, KEY_VALUE_HEADS, QUERY_PER_KEY), jnp.float32)
        numerator, weight_sum = lax.fori_loop(0, query_index + 1, accumulate, (initial_numerator, initial_sum))
        return (numerator / weight_sum[..., None]).astype(jnp.bfloat16).reshape(rows_per_block, QUERY_HEADS * HEAD_WIDTH)
    attended = lax.map(one_block, jnp.arange(count_of_blocks, dtype=jnp.int32)).reshape(TOKEN_COUNT, QUERY_HEADS * HEAD_WIDTH)
    return jnp.dot(attended, out_weight, preferred_element_type=jnp.float32).astype(jnp.bfloat16)
```

```python
import functools
import math

import jax
import jax.numpy as jnp
from jax import lax
from jax.experimental import pallas as pl
from jax.experimental.pallas import tpu as pltpu
from jax.sharding import Mesh, PartitionSpec as P

HEAD_WIDTH = 128
QUERY_PER_KEY = 8
BLOCK = 128
ROWS = 4096
TILE = 512
SUB = 256
LOG2_SCALE = math.log2(math.e) / math.sqrt(HEAD_WIDTH)
SCORE_LIMIT = 110.0
TOTAL_LANE = 128
SHIFT_LANE = 129
NONE = -1e30
VMEM_LIMIT = 48 * 2**20
X_COUNT, Z_COUNT = 4, 8


def dot_t(a, b):
    return lax.dot_general(a, b, (((1,), (1,)), ((), ())), preferred_element_type=jnp.float32)


def dot(a, b):
    return jnp.dot(a, b, preferred_element_type=jnp.float32)


def lane_iota(rows):
    return lax.broadcasted_iota(jnp.int32, (rows, 2 * HEAD_WIDTH), 1)


def stage_block(kv, visible, start, kk_ref, vv_ref):
    key = kv[:, :HEAD_WIDTH]
    value = kv[:, HEAD_WIDTH:]
    seen = visible.astype(jnp.float32)
    lane = lax.broadcasted_iota(jnp.int32, (BLOCK, HEAD_WIDTH), 1)
    ones = jnp.where(lane == 0, seen, 0.0).astype(jnp.bfloat16)
    value = jnp.where(jnp.broadcast_to(seen, value.shape) > 0.5, value.astype(jnp.float32), 0.0).astype(jnp.bfloat16)
    kk_ref[start : start + BLOCK, :HEAD_WIDTH] = key
    kk_ref[start : start + BLOCK, HEAD_WIDTH:] = key
    vv_ref[start : start + BLOCK, :HEAD_WIDTH] = value
    vv_ref[start : start + BLOCK, HEAD_WIDTH:] = ones
    wide = key.astype(jnp.float32)
    return jnp.max(jnp.sum(wide * wide, axis=1))


def key_spans(count):
    spans, at = [], 0
    while at < count:
        size = min(512, count - at)
        spans.append((at, size))
        at += size
    return spans


def fast_tile(count, q_ref, kk_ref, vv_ref, acc_in, mask):
    halves = range(TILE // SUB)
    rows = [pl.ds(h * SUB, SUB) for h in halves]
    query = [q_ref[r, :] for r in rows]
    total = [None if acc_in is None else acc_in[r, :] for r in rows]
    work = [(h, span) for span in key_spans(count) for h in halves]

    def scores(item):
        h, (at, size) = item
        return dot_t(query[h], kk_ref[at : at + size, :])

    now = scores(work[0])
    for place, (h, (at, size)) in enumerate(work):
        later = scores(work[place + 1]) if place + 1 < len(work) else None
        if mask is not None:
            now = jnp.where(mask(h * SUB, SUB, at, size), now, NONE)
        weights = jnp.exp2(now).astype(jnp.bfloat16)
        term = dot(weights, vv_ref[at : at + size, :])
        total[h] = term if total[h] is None else total[h] + term
        now = later
    return total


def slow_tile(count, q_ref, kk_ref, vv_ref, acc, mask):
    query = q_ref[...]

    def step(block, acc):
        at = pl.multiple_of(block * BLOCK, BLOCK)
        allowed = mask(0, TILE, at, BLOCK)
        scores = jnp.where(allowed, dot_t(query, kk_ref[pl.ds(at, BLOCK), :]), NONE)
        total = acc[:, TOTAL_LANE : TOTAL_LANE + 1]
        shift = jnp.where(total > 0.0, acc[:, SHIFT_LANE : SHIFT_LANE + 1], NONE)
        top = jnp.maximum(shift, jnp.max(scores, axis=1, keepdims=True))
        shift_now = jnp.where(top > 0.5 * NONE, top, 0.0)
        rescale = jnp.exp2(shift - shift_now)
        weights = jnp.where(allowed, jnp.exp2(scores - shift_now), 0.0).astype(jnp.bfloat16)
        acc = acc * rescale + dot(weights, vv_ref[pl.ds(at, BLOCK), :])
        return jnp.where(lane_iota(TILE) == SHIFT_LANE, shift_now, acc)

    return lax.fori_loop(0, count // BLOCK, step, acc)


def first_kernel(place_ref, q_ref, kv_ref, q2_ref, acc_ref, norm_ref, slow_ref, kk_ref, vv_ref, key_norm):
    step = pl.program_id(0)
    blocks = 2 * X_COUNT
    count = blocks * BLOCK

    @pl.when(step == 0)
    def _():
        largest = 0.0
        for b in range(blocks):
            part = kv_ref[b * BLOCK : (b + 1) * BLOCK, :]
            largest = jnp.maximum(largest, stage_block(part, jnp.int32(1), b * BLOCK, kk_ref, vv_ref))
        key_norm[0] = largest
        norm_ref[0] = 0.0
        slow_ref[0] = 0

    largest = 0.0
    for g in range(TILE // BLOCK):
        x = q_ref[0, :, g * HEAD_WIDTH : (g + 1) * HEAD_WIDTH].astype(jnp.float32) * LOG2_SCALE
        high = x.astype(jnp.bfloat16)
        q2_ref[g * BLOCK : (g + 1) * BLOCK, :HEAD_WIDTH] = high
        q2_ref[g * BLOCK : (g + 1) * BLOCK, HEAD_WIDTH:] = (x - high.astype(jnp.float32)).astype(jnp.bfloat16)
        largest = jnp.maximum(largest, jnp.max(jnp.sum(x * x, axis=1)))
    norm_ref[0] = jnp.maximum(norm_ref[0], largest)
    row_block = place_ref[step // 2]

    def mask(row_at, row_count, at, size):
        shape = (row_count, size)
        token = lax.broadcasted_iota(jnp.int32, shape, 0) % BLOCK + row_block * BLOCK
        lane = lax.broadcasted_iota(jnp.int32, (1, size), 1)
        key = jnp.zeros((1, size), jnp.int32)
        for b in range(size // BLOCK):
            index = 4 + at // BLOCK + b
            key = jnp.where(lane // BLOCK == b, place_ref[index] * BLOCK + lane % BLOCK, key)
        return jnp.broadcast_to(key, shape) <= token

    fits = largest * key_norm[0] <= SCORE_LIMIT**2

    @pl.when(fits)
    def _():
        total = fast_tile(count, q2_ref, kk_ref, vv_ref, None, mask)
        for h, value in enumerate(total):
            acc_ref[h * SUB : (h + 1) * SUB, :] = value

    @pl.when(jnp.logical_not(fits))
    def _():
        slow_ref[0] = 1
        acc_ref[...] = slow_tile(count, q2_ref, kk_ref, vv_ref, jnp.zeros((TILE, 2 * HEAD_WIDTH), jnp.float32), mask)


def split_bf16(x, terms):
    out = []
    for _ in range(terms):
        part = x.astype(jnp.bfloat16).astype(jnp.float32)
        out.append(part)
        x = x - part
    return out


def pack(acc):
    lane = lane_iota(acc.shape[0])
    terms = split_bf16(acc[:, TOTAL_LANE : TOTAL_LANE + 1], 3) + split_bf16(acc[:, SHIFT_LANE : SHIFT_LANE + 1], 3)
    out = jnp.where(lane < HEAD_WIDTH, acc, 0.0)
    for t, term in enumerate(terms):
        out = jnp.where(lane == HEAD_WIDTH + t, term, out)
    return out.astype(jnp.bfloat16)


def more_kernel(thresholds, sizes, packed, *refs):
    seen_ref, norm_ref, slow_in, q2_ref = refs[:4]
    kv_refs = refs[4 : 4 + len(sizes)]
    acc_in, acc_ref, slow_ref, kk_ref, vv_ref, flag = refs[4 + len(sizes) :]
    count = sum(sizes)

    @pl.when(pl.program_id(0) == 0)
    def _():
        largest = 0.0
        at = 0
        for kv_ref, size in zip(kv_refs, sizes):
            for b in range(size // BLOCK):
                part = kv_ref[b * BLOCK : (b + 1) * BLOCK, :]
                seen = (seen_ref[at // BLOCK] > 0).astype(jnp.int32)
                largest = jnp.maximum(largest, stage_block(part, seen, at, kk_ref, vv_ref))
                at += BLOCK
        fits = jnp.logical_and(slow_in[0] == 0, largest * norm_ref[0] <= SCORE_LIMIT**2)
        flag[0] = jnp.where(fits, 0, 1)
        slow_ref[0] = jnp.where(fits, 0, 1)

    def mask(row_at, row_count, at, size):
        return jnp.broadcast_to(seen_ref[at // BLOCK], (row_count, size)) > 0

    @pl.when(flag[0] == 0)
    def _():
        total = fast_tile(count, q2_ref, kk_ref, vv_ref, acc_in, None)
        for h, value in enumerate(total):
            acc_ref[h * SUB : (h + 1) * SUB, :] = pack(value) if packed else value

    @pl.when(flag[0] != 0)
    def _():
        value = slow_tile(count, q2_ref, kk_ref, vv_ref, acc_in[...], mask)
        acc_ref[...] = pack(value) if packed else value


SMEM = pl.BlockSpec(memory_space=pltpu.SMEM)
WHOLE = pl.BlockSpec(memory_space=pltpu.VMEM)


def estimate(rows, count):
    return pl.CostEstimate(
        flops=4 * rows * count * 2 * HEAD_WIDTH, bytes_accessed=rows * 2560, transcendentals=rows * count
    )


def attend_first(place, queries, kv):
    count = kv.shape[0]
    return pl.pallas_call(
        first_kernel,
        grid=(ROWS // TILE,),
        in_specs=[SMEM, pl.BlockSpec((1, BLOCK, 512), lambda i: (i // 2, 0, i % 2)), WHOLE],
        out_specs=[
            pl.BlockSpec((TILE, 256), lambda i: (i, 0)),
            pl.BlockSpec((TILE, 256), lambda i: (i, 0)),
            SMEM,
            SMEM,
        ],
        out_shape=[
            jax.ShapeDtypeStruct((ROWS, 256), jnp.bfloat16),
            jax.ShapeDtypeStruct((ROWS, 256), jnp.float32),
            jax.ShapeDtypeStruct((1,), jnp.float32),
            jax.ShapeDtypeStruct((1,), jnp.int32),
        ],
        scratch_shapes=[
            pltpu.VMEM((count, 256), jnp.bfloat16),
            pltpu.VMEM((count, 256), jnp.bfloat16),
            pltpu.SMEM((1,), jnp.float32),
        ],
        compiler_params=pltpu.CompilerParams(vmem_limit_bytes=VMEM_LIMIT),
        cost_estimate=estimate(ROWS, count),
        name="attend_first",
    )(place, queries, kv)


def attend_more(z, q2, state, pieces, rows=ROWS, first_row=0, packed=False):
    acc, norm, slow = state
    thresholds = [t for _, ts in pieces for t in ts]
    seen = (z >= jnp.array(thresholds, jnp.int32)).astype(jnp.int32)
    sizes = [a.shape[0] for a, _ in pieces]
    count = sum(sizes)
    skip = first_row // TILE
    tile_in = pl.BlockSpec((TILE, 256), lambda i: (i + skip, 0))
    whole = rows == ROWS
    acc_shift = skip if acc.shape[0] == ROWS else 0
    new, slow = pl.pallas_call(
        functools.partial(more_kernel, tuple(thresholds), tuple(sizes), packed),
        grid=(rows // TILE,),
        in_specs=[SMEM, SMEM, SMEM, tile_in]
        + [WHOLE] * len(pieces)
        + [pl.BlockSpec((TILE, 256), lambda i: (i + acc_shift, 0))],
        out_specs=[pl.BlockSpec((TILE, 256), lambda i: (i, 0)), SMEM],
        out_shape=[
            jax.ShapeDtypeStruct((rows, 256), jnp.bfloat16 if packed else jnp.float32),
            jax.ShapeDtypeStruct((1,), jnp.int32),
        ],
        scratch_shapes=[
            pltpu.VMEM((count, 256), jnp.bfloat16),
            pltpu.VMEM((count, 256), jnp.bfloat16),
            pltpu.SMEM((1,), jnp.int32),
        ],
        input_output_aliases={4 + len(pieces): 0} if whole else {},
        compiler_params=pltpu.CompilerParams(vmem_limit_bytes=VMEM_LIMIT),
        cost_estimate=estimate(rows, count),
        name="attend_more",
    )(seen, norm, slow, q2, *[a for a, _ in pieces], acc)
    return new, norm, slow


def project_kernel(place_ref, acc_ref, other_ref, w_ref, own_ref, rest_ref, att_ref):
    @pl.when(pl.program_id(0) == 0)
    def _():
        for y in range(2):
            for g in range(QUERY_PER_KEY):
                at = (y * QUERY_PER_KEY + g) * BLOCK
                here = acc_ref[at : at + BLOCK, :]
                there = other_ref[at : at + BLOCK, :].astype(jnp.float32)
                lanes = [there[:, HEAD_WIDTH + t : HEAD_WIDTH + t + 1] for t in range(6)]
                total_here = here[:, TOTAL_LANE : TOTAL_LANE + 1]
                total_there = lanes[0] + lanes[1] + lanes[2]
                shift_here = jnp.where(total_here > 0.0, here[:, SHIFT_LANE : SHIFT_LANE + 1], NONE)
                shift_there = jnp.where(total_there > 0.0, lanes[3] + lanes[4] + lanes[5], NONE)
                shift = jnp.maximum(shift_here, shift_there)
                scale_here = jnp.exp2(shift_here - shift)
                scale_there = jnp.exp2(shift_there - shift)
                total = total_here * scale_here + total_there * scale_there
                top = here[:, :HEAD_WIDTH] * scale_here + there[:, :HEAD_WIDTH] * scale_there
                att_ref[y * BLOCK : (y + 1) * BLOCK, g * HEAD_WIDTH : (g + 1) * HEAD_WIDTH] = (top / total).astype(
                    jnp.bfloat16
                )

    result = dot(att_ref[...], w_ref[...])
    res_ref = own_ref
    y = place_ref[1]
    half = BLOCK // 2
    parts = [result[r * half : (r + 1) * half, :] for r in range(4)]
    for d in range(4):
        target = (y + d) % 4
        picked = parts[0]
        for r in range(1, 4):
            picked = jnp.where(target == r, parts[r], picked)
        if d == 0:
            res_ref[...] = picked
        else:
            rest_ref[d - 1] = picked.astype(jnp.bfloat16)


def project(place, acc, other, weight):
    width = weight.shape[1]
    cut = 512
    half = BLOCK // 2
    return pl.pallas_call(
        project_kernel,
        grid_spec=pltpu.PrefetchScalarGridSpec(
            num_scalar_prefetch=1,
            grid=(width // cut,),
            in_specs=[
                WHOLE,
                WHOLE,
                pl.BlockSpec((QUERY_PER_KEY * HEAD_WIDTH, cut), lambda j, place: (place[0], j)),
            ],
            out_specs=[
                pl.BlockSpec((half, cut), lambda j, place: (0, j)),
                pl.BlockSpec((3, half, cut), lambda j, place: (0, 0, j)),
            ],
            scratch_shapes=[pltpu.VMEM((2 * BLOCK, QUERY_PER_KEY * HEAD_WIDTH), jnp.bfloat16)],
        ),
        out_shape=[
            jax.ShapeDtypeStruct((half, width), jnp.float32),
            jax.ShapeDtypeStruct((3, half, width), jnp.bfloat16),
        ],
        compiler_params=pltpu.CompilerParams(vmem_limit_bytes=VMEM_LIMIT),
        cost_estimate=pl.CostEstimate(
            flops=2 * 2 * BLOCK * 1024 * width, bytes_accessed=1024 * width * 2 + 2**22, transcendentals=4096
        ),
        name="project",
    )(place, acc, other, weight)


def body(queries, key_matrix, value_matrix, out_weight):
    z, yh, x, c, h = (lax.axis_index(a) for a in ("z", "yh", "x", "c", "h"))
    swap = [(0, 1), (1, 0)]
    first = yh == 0

    def pick(a, b):
        return jnp.where(first, a, b)

    def heads_of(a):
        half = a.shape[1] // 2
        return pick(a[:, :half], a[:, half:]), pick(a[:, half:], a[:, :half])

    key_mine, key_theirs = heads_of(key_matrix)
    value_mine, value_theirs = heads_of(value_matrix)
    kv_own = jnp.concatenate([key_mine, value_mine], axis=1)
    kv_partner = lax.ppermute(jnp.concatenate([key_theirs, value_theirs], axis=1), "yh", swap)

    own_z = [lax.ppermute(kv_own, "z", [(i, i + k) for i in range(Z_COUNT - k)]) for k in range(1, Z_COUNT)]

    q_mine, q_theirs = heads_of(queries)
    q_partner = lax.ppermute(q_theirs, "yh", swap)
    q_own = jnp.stack([pick(q_mine, q_partner), pick(q_partner, q_mine)])
    q_other = lax.ppermute(q_own, "c", swap)
    q_all = jnp.concatenate([q_own, q_other], axis=0)

    def around_x(a):
        moved = [lax.ppermute(a, "x", [(i, (i + s) % X_COUNT) for i in range(X_COUNT)]) for s in (1, 3, 2)]
        return moved

    both = jnp.concatenate([kv_own, kv_partner], axis=0)
    near = [both] + around_x(both)
    near_all = jnp.concatenate(near, axis=0)

    base = z * 16
    token_blocks = [base + y * 8 + x * 2 + cq for cq in (c, 1 - c) for y in (0, 1)]
    key_blocks = []
    for s in (0, 3, 1, 2):
        from_x = (x + s) % X_COUNT
        key_blocks += [base + yh * 8 + from_x * 2 + c, base + (1 - yh) * 8 + from_x * 2 + c]
    place = jnp.stack(token_blocks + key_blocks).astype(jnp.int32)

    ring = jnp.concatenate([n[BLOCK:] for n in near], axis=0)
    up, down = [], []
    up_now, down_now = ring, ring
    down_pairs = [[(0, 7), (1, 0), (2, 1)], [(0, 7), (7, 6), (1, 0)], [(0, 7), (7, 6), (6, 5)]]
    for s in range(1, 5):
        up_now = lax.ppermute(up_now, "z", [(i, i + 1) for i in range(s - 1, Z_COUNT - 1)])
        up.append(up_now)
        if s < 4:
            down_now = lax.ppermute(down_now, "z", down_pairs[s - 1])
            down.append(down_now)

    column = jnp.concatenate(own_z, axis=0)
    column_left, column_right, column_far = around_x(column)

    def ring_piece(array, k):
        return (array, [k] * X_COUNT)

    def column_piece(array):
        return (array, list(range(1, Z_COUNT)))

    q2, acc, norm, slow = attend_first(place, q_all, near_all)
    state = (acc, norm, slow)
    state = attend_more(z, q2, state, [column_piece(column), ring_piece(up[0], 1), ring_piece(down[0], 7)])
    state = attend_more(z, q2, state, [ring_piece(up[1], 2), ring_piece(down[1], 6), column_piece(column_left)])
    state = attend_more(z, q2, state, [ring_piece(up[2], 3), ring_piece(down[2], 5), column_piece(column_right)])
    last = [ring_piece(up[3], 4), column_piece(column_far)]
    half = ROWS // 2
    sent, _, _ = attend_more(z, q2, state, last, rows=half, first_row=half, packed=True)
    other = lax.ppermute(sent, "c", swap)
    mine, _, _ = attend_more(z, q2, state, last, rows=half, first_row=0)

    where = jnp.stack([yh, yh * 2 + h]).astype(jnp.int32)
    own, rest = project(where, mine, other, out_weight)
    out = own
    for d in (2, 1, 3):
        out = out + lax.ppermute(rest[d - 1], ("yh", "h"), [(i, (i + d) % 4) for i in range(4)]).astype(jnp.float32)
    return out.astype(jnp.bfloat16)


def solution(mesh):
    split = Mesh(mesh.devices.reshape(Z_COUNT, 2, X_COUNT, 2, 2), ("z", "yh", "x", "c", "h"))
    tokens = ("z", "yh", "x", "c")
    return jax.shard_map(
        body,
        mesh=split,
        in_specs=(P(tokens, "h"), P(tokens, "h"), P(tokens, "h"), P("h", None)),
        out_specs=P(tokens + ("h",), None),
        check_vma=False,
    )
```

```python
import functools
import math

import jax
import jax.numpy as jnp
from jax import lax
from jax.experimental import pallas as pl
from jax.experimental.pallas import tpu as pltpu
from jax.sharding import Mesh, PartitionSpec as P

HEAD_WIDTH = 128
QUERY_PER_KEY = 8
BLOCK = 128
ROWS = 4096
TILE = 1024
SUB = 256
LOG2_SCALE = math.log2(math.e) / math.sqrt(HEAD_WIDTH)
SCORE_LIMIT = 110.0
TOTAL_LANE = 128
SHIFT_LANE = 129
NONE = -1e30
VMEM_LIMIT = 16 * 2**20
X_COUNT, Z_COUNT = 4, 8
COST = 6


def dot_t(a, b):
    return lax.dot_general(a, b, (((1,), (1,)), ((), ())), preferred_element_type=jnp.float32)


def dot(a, b):
    return jnp.dot(a, b, preferred_element_type=jnp.float32)


def lane_iota(rows):
    return lax.broadcasted_iota(jnp.int32, (rows, 2 * HEAD_WIDTH), 1)


def squared_norms(a):
    norms = dot(a * a, jnp.full((HEAD_WIDTH, HEAD_WIDTH), 1.0, jnp.bfloat16))
    return jnp.max(norms, axis=0, keepdims=True) * 1.02


def stage_block(kv, start, kk_ref, vv_ref):
    key = kv[:, :HEAD_WIDTH]
    lane = lax.broadcasted_iota(jnp.int32, (BLOCK, HEAD_WIDTH), 1)
    rows = pl.ds(start, BLOCK)
    kk_ref[rows, :HEAD_WIDTH] = key
    kk_ref[rows, HEAD_WIDTH:] = key
    vv_ref[rows, :HEAD_WIDTH] = kv[:, HEAD_WIDTH:]
    vv_ref[rows, HEAD_WIDTH:] = jnp.where(lane == 0, 1.0, 0.0).astype(jnp.bfloat16)
    return squared_norms(key)


def key_spans(count):
    spans, at = [], 0
    while at < count:
        size = min(512, count - at)
        spans.append((at, size))
        at += size
    return spans


def fast_tile(counts, q_ref, kk_ref, vv_ref, acc_in, mask, store):
    work = [(r, span, count) for r, count in enumerate(counts) for span in key_spans(count)]

    def scores(item):
        r, (at, size), _ = item
        return dot_t(q_ref[r * SUB : (r + 1) * SUB, :], kk_ref[at : at + size, :])

    now = scores(work[0])
    total = None
    for index, (r, (at, size), count) in enumerate(work):
        later = scores(work[index + 1]) if index + 1 < len(work) else None
        if mask is not None and at + size == count:
            now = jnp.where(mask(r * SUB, SUB, at, size), now, NONE)
        weights = jnp.exp2(now).astype(jnp.bfloat16)
        term = dot(weights, vv_ref[at : at + size, :])
        total = term if total is None else total + term
        if at + size == count:
            if acc_in is not None:
                total = acc_in[r * SUB : (r + 1) * SUB, :] + total
            store(r * SUB, total)
            total = None
        now = later


def slow_tile(blocks, q_ref, kk_ref, vv_ref, acc, mask=None):
    query = q_ref[...]

    def step(block, acc):
        at = pl.multiple_of(block * BLOCK, BLOCK)
        scores = dot_t(query, kk_ref[pl.ds(at, BLOCK), :])
        if mask is not None:
            allowed = mask(0, TILE, at, BLOCK)
            scores = jnp.where(allowed, scores, NONE)
        total = acc[:, TOTAL_LANE : TOTAL_LANE + 1]
        shift = jnp.where(total > 0.0, acc[:, SHIFT_LANE : SHIFT_LANE + 1], NONE)
        top = jnp.maximum(shift, jnp.max(scores, axis=1, keepdims=True))
        shift_now = jnp.where(top > 0.5 * NONE, top, 0.0)
        rescale = jnp.exp2(shift - shift_now)
        weights = jnp.exp2(scores - shift_now)
        if mask is not None:
            weights = jnp.where(allowed, weights, 0.0)
        weights = weights.astype(jnp.bfloat16)
        acc = acc * rescale + dot(weights, vv_ref[pl.ds(at, BLOCK), :])
        return jnp.where(lane_iota(TILE) == SHIFT_LANE, shift_now, acc)

    return lax.fori_loop(0, blocks, step, acc)


def put_info(info_ref, norm, slow):
    row = lax.broadcasted_iota(jnp.int32, (8, HEAD_WIDTH), 0)
    info_ref[...] = jnp.where(row == 0, norm, jnp.where(row == 1, slow, 0.0))


def prepare_kernel(own_ref, other_ref, q2_ref, info_ref):
    h = lax.axis_index("h")
    norms = []
    half = BLOCK // 2
    at = 0
    for q_ref in (own_ref, other_ref):
        for kept in (1 - h, h):
            rows = pl.ds(pl.multiple_of(kept * half, half), half)
            for y in range(2):
                for g in range(QUERY_PER_KEY):
                    wide = q_ref[y, rows, g * HEAD_WIDTH : (g + 1) * HEAD_WIDTH].astype(jnp.float32) * LOG2_SCALE
                    high = wide.astype(jnp.bfloat16)
                    q2_ref[at : at + half, :HEAD_WIDTH] = high
                    q2_ref[at : at + half, HEAD_WIDTH:] = (wide - high.astype(jnp.float32)).astype(jnp.bfloat16)
                    norms.append(squared_norms(high))
                    at += half
    put_info(info_ref, functools.reduce(jnp.maximum, norms) * 1.02, 0.0)


def own_mask(tile, h, yh, x, c):
    half = BLOCK // 2
    core = jnp.where(tile < 2, c, 1 - c)
    kept = jnp.where(tile % 2 == 0, 1 - h, h)

    def mask(row_at, row_count, at, size):
        shape = (row_count, size)
        row = lax.broadcasted_iota(jnp.int32, shape, 0) + row_at
        row_y = jnp.where(row < TILE // 2, yh, 1 - yh)
        token = row % half + (row_y * 8 + x * 2 + core) * BLOCK + kept * half
        lane = lax.broadcasted_iota(jnp.int32, (1, size), 1)
        key = jnp.zeros((1, size), jnp.int32)
        for b in range(size // BLOCK):
            block = at // BLOCK + b
            slot = block % X_COUNT
            back = jnp.where(slot == 1, 3, jnp.where(slot == 2, 1, jnp.where(slot == 3, 2, 0)))
            from_x = (x + back) % X_COUNT
            token_of = ((block // X_COUNT) * 8 + from_x * 2 + c) * BLOCK
            key = jnp.where(lane // BLOCK == b, token_of + lane % BLOCK, key)
        return jnp.broadcast_to(key, shape) <= token

    return mask


def first_kernel(*refs):
    info_in, q2_ref = refs[:2]
    kv_refs = refs[2 : 2 + X_COUNT]
    acc_ref, info_ref, kk_ref, vv_ref, flag = refs[2 + X_COUNT :]
    yh, x, c = lax.axis_index("yh"), lax.axis_index("x"), lax.axis_index("c")
    half = X_COUNT * BLOCK
    count = 2 * half

    @pl.when(pl.program_id(0) == 0)
    def _():
        bounds = []
        for s, kv_ref in enumerate(kv_refs):
            for partner in range(2):
                y = yh if partner == 0 else 1 - yh
                start = pl.multiple_of(y * half + s * BLOCK, BLOCK)
                bounds.append(stage_block(kv_ref[partner * BLOCK : (partner + 1) * BLOCK, :], start, kk_ref, vv_ref))
        fits = jnp.max(functools.reduce(jnp.maximum, bounds) * info_in[0:1, :]) <= SCORE_LIMIT**2
        flag[0] = jnp.where(fits, 0, 1)
        put_info(info_ref, info_in[0:1, :], jnp.where(fits, 0.0, 1.0))

    mask = own_mask(pl.program_id(0), lax.axis_index("h"), yh, x, c)

    def store(at, value):
        acc_ref[at : at + SUB, :] = value

    subs = TILE // SUB // 2
    for y in range(2):

        @pl.when(jnp.logical_and(flag[0] == 0, yh == y))
        def _(y=y):
            counts = [half * (1 + y)] * subs + [half * (2 - y)] * subs
            fast_tile(counts, q2_ref, kk_ref, vv_ref, None, mask, store)

    @pl.when(flag[0] != 0)
    def _():
        acc = jnp.zeros((TILE, 2 * HEAD_WIDTH), jnp.float32)
        acc_ref[...] = slow_tile(count // BLOCK, q2_ref, kk_ref, vv_ref, acc, mask)


def pack(acc):
    shape = (acc.shape[0], HEAD_WIDTH)
    lane = lax.broadcasted_iota(jnp.int32, shape, 1)
    right = jnp.zeros(shape, jnp.float32)
    for first, source in ((0, TOTAL_LANE), (3, SHIFT_LANE)):
        left = jnp.broadcast_to(acc[:, source : source + 1], shape)
        for t in range(3):
            term = left.astype(jnp.bfloat16).astype(jnp.float32)
            right = jnp.where(lane == first + t, term, right)
            left = left - term
    return jnp.concatenate([acc[:, :HEAD_WIDTH].astype(jnp.bfloat16), right.astype(jnp.bfloat16)], axis=1)


def unpack_matrix():
    shape = (2 * HEAD_WIDTH, 3 * HEAD_WIDTH)
    row = lax.broadcasted_iota(jnp.int32, shape, 0)
    column = lax.broadcasted_iota(jnp.int32, shape, 1)
    part = column // HEAD_WIDTH
    numerator = jnp.logical_and(part == 0, row == column)
    term = (row - HEAD_WIDTH) // 3 == part - 1
    term = jnp.logical_and(term, jnp.logical_and(row >= HEAD_WIDTH, part > 0))
    return jnp.where(jnp.logical_or(numerator, term), 1.0, 0.0).astype(jnp.bfloat16)


def more_kernel(needed, sizes, packed, *refs):
    info_in, q2_ref = refs[:2]
    kv_refs = refs[2 : 2 + len(sizes)]
    acc_in, acc_ref, info_ref, kk_ref, vv_ref, key_norm, flag = refs[2 + len(sizes) :]
    z = lax.axis_index("z")
    ends = [sum(sizes[: i + 1]) for i in range(len(sizes))]
    levels = {}
    for least, end in zip(needed, ends):
        levels[least] = end
    steps = sorted(levels)

    @pl.when(pl.program_id(0) == 0)
    def _():
        key_norm[...] = jnp.zeros_like(key_norm)
        for least in steps:

            @pl.when(z >= least)
            def _(least=least):
                bounds = []
                for kv_ref, size, end, own in zip(kv_refs, sizes, ends, needed):
                    for b in range(size // BLOCK if own == least else 0):
                        part = kv_ref[b * BLOCK : (b + 1) * BLOCK, :]
                        bounds.append(stage_block(part, end - size + b * BLOCK, kk_ref, vv_ref))
                key_norm[0:1, :] = jnp.maximum(key_norm[0:1, :], functools.reduce(jnp.maximum, bounds))

        bound = jnp.where(info_in[1:2, :] > 0.5, 2.0 * SCORE_LIMIT**2, info_in[0:1, :] * key_norm[0:1, :])
        fits = jnp.max(bound) <= SCORE_LIMIT**2
        flag[0] = jnp.where(fits, 0, 1)
        put_info(info_ref, info_in[0:1, :], jnp.where(fits, 0.0, 1.0))

    def store(at, value):
        acc_ref[at : at + SUB, :] = pack(value) if packed else value

    @pl.when(z < steps[0])
    def _():
        for at in range(0, TILE, SUB):
            store(at, acc_in[at : at + SUB, :])

    for index, least in enumerate(steps):
        here = z >= least
        if index + 1 < len(steps):
            here = jnp.logical_and(here, z < steps[index + 1])

        @pl.when(jnp.logical_and(here, flag[0] == 0))
        def _(least=least):
            fast_tile([levels[least]] * (TILE // SUB), q2_ref, kk_ref, vv_ref, acc_in, None, store)

    @pl.when(jnp.logical_and(z >= steps[0], flag[0] != 0))
    def _():
        blocks = jnp.int32(0)
        for least in steps:
            blocks = jnp.where(z >= least, levels[least] // BLOCK, blocks)
        value = slow_tile(blocks, q2_ref, kk_ref, vv_ref, acc_in[...])
        acc_ref[...] = pack(value) if packed else value


WHOLE = pl.BlockSpec(memory_space=pltpu.VMEM)


def estimate(rows, count):
    return pl.CostEstimate(
        flops=COST * 4 * rows * count * 2 * HEAD_WIDTH, bytes_accessed=rows * 2560, transcendentals=rows * count
    )


INFO = jax.ShapeDtypeStruct((8, HEAD_WIDTH), jnp.float32)


def prepare(own, other):
    return pl.pallas_call(
        prepare_kernel,
        in_specs=[WHOLE] * 2,
        out_specs=[WHOLE] * 2,
        out_shape=[jax.ShapeDtypeStruct((ROWS, 256), jnp.bfloat16), INFO],
        compiler_params=pltpu.CompilerParams(vmem_limit_bytes=VMEM_LIMIT),
        cost_estimate=pl.CostEstimate(flops=ROWS * 2**15, bytes_accessed=ROWS * 768, transcendentals=0),
        name="prepare",
    )(own, other)


def attend_first(q2, info, pieces):
    count = sum(a.shape[0] for a in pieces)
    return pl.pallas_call(
        first_kernel,
        grid=(ROWS // TILE,),
        in_specs=[WHOLE, pl.BlockSpec((TILE, 256), lambda i: (i, 0))] + [WHOLE] * len(pieces),
        out_specs=[pl.BlockSpec((TILE, 256), lambda i: (i, 0)), WHOLE],
        out_shape=[jax.ShapeDtypeStruct((ROWS, 256), jnp.float32), INFO],
        scratch_shapes=[pltpu.VMEM((count, 256), jnp.bfloat16)] * 2 + [pltpu.SMEM((1,), jnp.int32)],
        compiler_params=pltpu.CompilerParams(vmem_limit_bytes=VMEM_LIMIT),
        cost_estimate=estimate(ROWS, count),
        name="attend_first",
    )(info, q2, *pieces)


def attend_more(q2, state, pieces, rows=ROWS, first_row=0, packed=False):
    acc, info = state
    pieces = sorted(pieces, key=lambda piece: piece[1])
    needed = [least for _, least in pieces]
    sizes = [a.shape[0] for a, _ in pieces]
    count = sum(sizes)
    skip = first_row // TILE
    whole = rows == ROWS
    tile_in = pl.BlockSpec((TILE, 256), lambda i: (i + skip, 0))
    return pl.pallas_call(
        functools.partial(more_kernel, tuple(needed), tuple(sizes), packed),
        grid=(rows // TILE,),
        in_specs=[WHOLE, tile_in] + [WHOLE] * len(pieces) + [tile_in],
        out_specs=[pl.BlockSpec((TILE, 256), lambda i: (i, 0)), WHOLE],
        out_shape=[jax.ShapeDtypeStruct((rows, 256), jnp.bfloat16 if packed else jnp.float32), INFO],
        scratch_shapes=[
            pltpu.VMEM((count, 256), jnp.bfloat16),
            pltpu.VMEM((count, 256), jnp.bfloat16),
            pltpu.VMEM((8, HEAD_WIDTH), jnp.float32),
            pltpu.SMEM((1,), jnp.int32),
        ],
        input_output_aliases={2 + len(pieces): 0} if whole else {},
        compiler_params=pltpu.CompilerParams(vmem_limit_bytes=VMEM_LIMIT),
        cost_estimate=estimate(rows, count),
        name="attend_more",
    )(info, q2, *[a for a, _ in pieces], acc)


def project_kernel(kept, yh_ref, acc_ref, other_ref, w_ref, *refs):
    *out_refs, att_ref = refs
    half = BLOCK // 2

    @pl.when(pl.program_id(0) == 0)
    def _():
        matrix = unpack_matrix()
        shape = (half, HEAD_WIDTH)
        for y in range(2):
            for g in range(QUERY_PER_KEY):
                at = (y * QUERY_PER_KEY + g) * half
                here = acc_ref[at : at + half, :]
                there = dot(other_ref[at : at + half, :], matrix)
                total_here = jnp.broadcast_to(here[:, TOTAL_LANE : TOTAL_LANE + 1], shape)
                total_there = there[:, HEAD_WIDTH : 2 * HEAD_WIDTH]
                shift_here = jnp.broadcast_to(here[:, SHIFT_LANE : SHIFT_LANE + 1], shape)
                shift_here = jnp.where(total_here > 0.0, shift_here, NONE)
                shift_there = jnp.where(total_there > 0.0, there[:, 2 * HEAD_WIDTH :], NONE)
                shift = jnp.maximum(shift_here, shift_there)
                scale_here = jnp.exp2(shift_here - shift)
                scale_there = jnp.exp2(shift_there - shift)
                total = total_here * scale_here + total_there * scale_there
                top = here[:, :HEAD_WIDTH] * scale_here + there[:, :HEAD_WIDTH] * scale_there
                att_ref[y * half : (y + 1) * half, g * HEAD_WIDTH : (g + 1) * HEAD_WIDTH] = (top / total).astype(
                    jnp.bfloat16
                )

    result = dot(att_ref[...], w_ref[...])
    mine, partner = result[:half, :], result[half:, :]
    if kept:
        out_refs[0][...] = mine
        out_refs[1][...] = partner.astype(jnp.bfloat16)
    else:
        even = lax.axis_index("h") == 0
        out_refs[0][...] = jnp.where(even, mine, partner).astype(jnp.bfloat16)
        out_refs[1][...] = jnp.where(even, partner, mine).astype(jnp.bfloat16)


def project(yh, acc, other, other_row, weight, kept):
    width = weight.shape[1]
    cut = 512
    half = BLOCK // 2
    tile = other_row // TILE
    return pl.pallas_call(
        functools.partial(project_kernel, kept),
        grid_spec=pltpu.PrefetchScalarGridSpec(
            num_scalar_prefetch=1,
            grid=(width // cut,),
            in_specs=[
                WHOLE,
                pl.BlockSpec((TILE, 256), lambda j, yh: (tile, 0)),
                pl.BlockSpec((QUERY_PER_KEY * HEAD_WIDTH, cut), lambda j, yh: (yh[0], j)),
            ],
            out_specs=[pl.BlockSpec((half, cut), lambda j, yh: (0, j))] * 2,
            scratch_shapes=[pltpu.VMEM((BLOCK, QUERY_PER_KEY * HEAD_WIDTH), jnp.bfloat16)],
        ),
        out_shape=[
            jax.ShapeDtypeStruct((half, width), jnp.float32 if kept else jnp.bfloat16),
            jax.ShapeDtypeStruct((half, width), jnp.bfloat16),
        ],
        compiler_params=pltpu.CompilerParams(vmem_limit_bytes=VMEM_LIMIT),
        cost_estimate=pl.CostEstimate(
            flops=COST * 2 * BLOCK * 1024 * width, bytes_accessed=1024 * width * 2 + 2**21, transcendentals=2048
        ),
        name="project",
    )(yh, acc, other, weight)


def body(queries, key_matrix, value_matrix, out_weight):
    yh = lax.axis_index("yh")
    swap = [(0, 1), (1, 0)]
    first = yh == 0

    def pick(a, b):
        return jnp.where(first, a, b)

    def heads_of(a):
        half = a.shape[1] // 2
        return pick(a[:, :half], a[:, half:]), pick(a[:, half:], a[:, :half])

    key_mine, key_theirs = heads_of(key_matrix)
    value_mine, value_theirs = heads_of(value_matrix)
    kv_own = jnp.concatenate([key_mine, value_mine], axis=1)
    kv_theirs, kv_own, queries = lax.optimization_barrier(
        (jnp.concatenate([key_theirs, value_theirs], axis=1), kv_own, queries)
    )
    kv_partner = lax.ppermute(kv_theirs, "yh", swap)

    q_mine, q_theirs = heads_of(queries)
    kv_partner, q_theirs = lax.optimization_barrier((kv_partner, q_theirs))
    q_partner = lax.ppermute(q_theirs, "yh", swap)
    both = jnp.concatenate([kv_own, kv_partner], axis=0)

    def around_x(a):
        moved = [lax.ppermute(a, "x", [(i, (i + s) % X_COUNT) for i in range(X_COUNT)]) for s in (1, 3, 2)]
        return moved

    near = [both] + around_x(both)

    ring, q_mine = lax.optimization_barrier((jnp.concatenate(near, axis=0), q_mine))
    q_own = jnp.stack([q_mine, q_partner])
    q2, info = prepare(q_own, lax.ppermute(q_own, "c", swap))
    half = ring.shape[0] // 2
    down_pairs = [
        [(0, 7), (1, 0), (2, 1), (3, 2)],
        [(0, 7), (7, 6), (1, 0), (2, 1)],
        [(0, 7), (7, 6), (6, 5), (1, 0)],
        [(0, 7), (7, 6), (6, 5), (5, 4)],
    ]

    def around_z(up, down, s):
        up = lax.ppermute(up, "z", [(i, i + 1) for i in range(s - 1, Z_COUNT - 1)])
        return up, lax.ppermute(down, "z", down_pairs[s - 1])

    def pieces(pair, s):
        return list(zip(pair, (s, Z_COUNT - s)))

    state = attend_first(q2, info, near)
    pair = around_z(ring, ring, 1)
    for s in (1, 2, 3):
        up, down, info = lax.optimization_barrier((*pair, state[1]))
        state = (state[0], info)
        if s < 3:
            later = around_z(up, down, s + 1)
        else:
            later = around_z(up[:half], down[half:], s + 1)
        state = attend_more(q2, state, pieces((up, down), s))
        pair = later
    last = pieces(pair, 4)
    rows = ROWS // 2
    sent, _ = attend_more(q2, state, last, rows=rows, first_row=rows, packed=True)
    other = lax.ppermute(sent, "c", swap)
    far, _ = attend_more(q2, state, last, rows=TILE, first_row=0)
    place = yh.reshape(1).astype(jnp.int32)
    to_next, to_previous = project(place, far, other, 0, out_weight, False)

    def on_y(a, d):
        return lax.ppermute(a, ("yh", "h"), [(i, (i + d) % 4) for i in range(4)])

    parts = [on_y(to_next, 1), on_y(to_previous, 3)]
    near_by, _ = attend_more(q2, state, last, rows=TILE, first_row=TILE)
    own, to_partner = project(place, near_by, other, TILE, out_weight, True)
    parts.append(on_y(to_partner, 2))
    out = own
    for part in parts:
        out = out + part.astype(jnp.float32)
    return out.astype(jnp.bfloat16)


def solution(mesh):
    split = Mesh(mesh.devices.reshape(Z_COUNT, 2, X_COUNT, 2, 2), ("z", "yh", "x", "c", "h"))
    tokens = ("z", "yh", "x", "c")
    return jax.shard_map(
        body,
        mesh=split,
        in_specs=(P(tokens, "h"), P(tokens, "h"), P(tokens, "h"), P("h", None)),
        out_specs=P(tokens + ("h",), None),
        check_vma=False,
    )
```

```python
import functools
import math

import jax
import jax.numpy as jnp
from jax import lax
from jax.experimental import pallas as pl
from jax.experimental.pallas import tpu as pltpu
from jax.sharding import Mesh, PartitionSpec as P

HEAD_WIDTH = 128
QUERY_PER_KEY = 8
BLOCK = 128
ROWS = 4096
TILE = 1024
SUB = 256
LOG2_SCALE = math.log2(math.e) / math.sqrt(HEAD_WIDTH)
SCORE_LIMIT = 110.0
TOTAL_LANE = 128
SHIFT_LANE = 131
NONE = -1e30
VMEM_LIMIT = 16 * 2**20
X_COUNT, Z_COUNT = 4, 8
COST = 6


def dot_t(a, b):
    return lax.dot_general(a, b, (((1,), (1,)), ((), ())), preferred_element_type=jnp.float32)


def dot(a, b):
    return jnp.dot(a, b, preferred_element_type=jnp.float32)


def lane_iota(rows):
    return lax.broadcasted_iota(jnp.int32, (rows, 2 * HEAD_WIDTH), 1)


def squared_norms(a):
    norms = dot(a * a, jnp.full((HEAD_WIDTH, HEAD_WIDTH), 1.0, jnp.bfloat16))
    return jnp.max(norms, axis=0, keepdims=True) * 1.02


def stage_block(kv, start, kk_ref, vv_ref):
    key = kv[:, :HEAD_WIDTH]
    lane = lax.broadcasted_iota(jnp.int32, (BLOCK, HEAD_WIDTH), 1)
    rows = pl.ds(start, BLOCK)
    kk_ref[rows, :HEAD_WIDTH] = key
    kk_ref[rows, HEAD_WIDTH:] = key
    vv_ref[rows, :HEAD_WIDTH] = kv[:, HEAD_WIDTH:]
    vv_ref[rows, HEAD_WIDTH:] = jnp.where(lane < 3, 1.0, 0.0).astype(jnp.bfloat16)
    return squared_norms(key)


def key_spans(count):
    spans, at = [], 0
    while at < count:
        size = min(512, count - at)
        spans.append((at, size))
        at += size
    return spans


def fast_tile(counts, q_ref, kk_ref, vv_ref, acc_in, mask, store):
    work = [(r, span, count) for r, count in enumerate(counts) for span in key_spans(count)]

    def scores(item):
        r, (at, size), _ = item
        return dot_t(q_ref[r * SUB : (r + 1) * SUB, :], kk_ref[at : at + size, :])

    now = scores(work[0])
    total = None
    for index, (r, (at, size), count) in enumerate(work):
        later = scores(work[index + 1]) if index + 1 < len(work) else None
        if mask is not None and at + size == count:
            now = jnp.where(mask(r * SUB, SUB, at, size), now, NONE)
        weights = jnp.exp2(now).astype(jnp.bfloat16)
        term = dot(weights, vv_ref[at : at + size, :])
        total = term if total is None else total + term
        if at + size == count:
            if acc_in is not None:
                total = acc_in[r * SUB : (r + 1) * SUB, :] + total
            store(r * SUB, total)
            total = None
        now = later


def slow_tile(blocks, q_ref, kk_ref, vv_ref, acc, mask=None):
    query = q_ref[...]

    def step(block, acc):
        at = pl.multiple_of(block * BLOCK, BLOCK)
        scores = dot_t(query, kk_ref[pl.ds(at, BLOCK), :])
        if mask is not None:
            allowed = mask(0, TILE, at, BLOCK)
            scores = jnp.where(allowed, scores, NONE)
        total = acc[:, TOTAL_LANE : TOTAL_LANE + 1]
        shift = jnp.where(total > 0.0, acc[:, SHIFT_LANE : SHIFT_LANE + 1], NONE)
        top = jnp.maximum(shift, jnp.max(scores, axis=1, keepdims=True))
        shift_now = jnp.where(top > 0.5 * NONE, top, 0.0)
        rescale = jnp.exp2(shift - shift_now)
        weights = jnp.exp2(scores - shift_now)
        if mask is not None:
            weights = jnp.where(allowed, weights, 0.0)
        weights = weights.astype(jnp.bfloat16)
        acc = acc * rescale + dot(weights, vv_ref[pl.ds(at, BLOCK), :])
        return jnp.where(lane_iota(TILE) == SHIFT_LANE, shift_now, acc)

    return lax.fori_loop(0, blocks, step, acc)


def put_info(info_ref, norm, slow):
    row = lax.broadcasted_iota(jnp.int32, (8, HEAD_WIDTH), 0)
    info_ref[...] = jnp.where(row == 0, norm, jnp.where(row == 1, slow, 0.0))


def prepare_kernel(*refs):
    q2_ref, info_ref = refs[4:]
    h = lax.axis_index("h")
    norms = []
    half = BLOCK // 2
    at = 0
    for q_refs in (refs[:2], refs[2:4]):
        for kept in (1 - h, h):
            rows = pl.ds(pl.multiple_of(kept * half, half), half)
            for q_ref in q_refs:
                for g in range(QUERY_PER_KEY):
                    wide = q_ref[rows, g * HEAD_WIDTH : (g + 1) * HEAD_WIDTH].astype(jnp.float32) * LOG2_SCALE
                    high = wide.astype(jnp.bfloat16)
                    q2_ref[at : at + half, :HEAD_WIDTH] = high
                    q2_ref[at : at + half, HEAD_WIDTH:] = (wide - high.astype(jnp.float32)).astype(jnp.bfloat16)
                    norms.append(squared_norms(high))
                    at += half
    put_info(info_ref, functools.reduce(jnp.maximum, norms) * 1.02, 0.0)


def own_mask(tile, h, yh, x, c):
    half = BLOCK // 2
    core = jnp.where(tile < 2, c, 1 - c)
    kept = jnp.where(tile % 2 == 0, 1 - h, h)

    def mask(row_at, row_count, at, size):
        shape = (row_count, size)
        row = lax.broadcasted_iota(jnp.int32, shape, 0) + row_at
        row_y = jnp.where(row < TILE // 2, yh, 1 - yh)
        token = row % half + (row_y * 8 + x * 2 + core) * BLOCK + kept * half
        lane = lax.broadcasted_iota(jnp.int32, (1, size), 1)
        key = jnp.zeros((1, size), jnp.int32)
        for b in range(size // BLOCK):
            block = at // BLOCK + b
            slot = block % X_COUNT
            back = jnp.where(slot == 1, 3, jnp.where(slot == 2, 1, jnp.where(slot == 3, 2, 0)))
            from_x = (x + back) % X_COUNT
            token_of = ((block // X_COUNT) * 8 + from_x * 2 + c) * BLOCK
            key = jnp.where(lane // BLOCK == b, token_of + lane % BLOCK, key)
        return jnp.broadcast_to(key, shape) <= token

    return mask


def first_kernel(*refs):
    info_in, q2_ref = refs[:2]
    kv_refs = refs[2 : 2 + X_COUNT]
    acc_ref, info_ref, kk_ref, vv_ref, flag = refs[2 + X_COUNT :]
    yh, x, c = lax.axis_index("yh"), lax.axis_index("x"), lax.axis_index("c")
    half = X_COUNT * BLOCK
    count = 2 * half

    @pl.when(pl.program_id(0) == 0)
    def _():
        bounds = []
        for s, kv_ref in enumerate(kv_refs):
            for partner in range(2):
                y = yh if partner == 0 else 1 - yh
                start = pl.multiple_of(y * half + s * BLOCK, BLOCK)
                bounds.append(stage_block(kv_ref[partner * BLOCK : (partner + 1) * BLOCK, :], start, kk_ref, vv_ref))
        fits = jnp.max(functools.reduce(jnp.maximum, bounds) * info_in[0:1, :]) <= SCORE_LIMIT**2
        flag[0] = jnp.where(fits, 0, 1)
        put_info(info_ref, info_in[0:1, :], jnp.where(fits, 0.0, 1.0))

    mask = own_mask(pl.program_id(0), lax.axis_index("h"), yh, x, c)

    def store(at, value):
        acc_ref[at : at + SUB, :] = value

    subs = TILE // SUB // 2
    for y in range(2):

        @pl.when(jnp.logical_and(flag[0] == 0, yh == y))
        def _(y=y):
            counts = [half * (1 + y)] * subs + [half * (2 - y)] * subs
            fast_tile(counts, q2_ref, kk_ref, vv_ref, None, mask, store)

    @pl.when(flag[0] != 0)
    def _():
        acc = jnp.zeros((TILE, 2 * HEAD_WIDTH), jnp.float32)
        acc_ref[...] = slow_tile(count // BLOCK, q2_ref, kk_ref, vv_ref, acc, mask)


def pack(acc, shifted):
    shape = (acc.shape[0], HEAD_WIDTH)
    lane = lax.broadcasted_iota(jnp.int32, shape, 1)
    left = acc[:, HEAD_WIDTH:]
    if shifted:
        shift = jnp.broadcast_to(acc[:, SHIFT_LANE : SHIFT_LANE + 1], shape)
        left = jnp.where(jnp.logical_and(lane >= 3, lane < 6), shift, left)
    right = jnp.zeros(shape, jnp.float32)
    for t in range(3):
        term = left.astype(jnp.bfloat16).astype(jnp.float32)
        right = jnp.where(jnp.logical_or(lane == t, lane == 3 + t), term, right)
        left = left - term
    return jnp.concatenate([acc[:, :HEAD_WIDTH].astype(jnp.bfloat16), right.astype(jnp.bfloat16)], axis=1)


def unpack_matrix():
    shape = (2 * HEAD_WIDTH, 3 * HEAD_WIDTH)
    row = lax.broadcasted_iota(jnp.int32, shape, 0)
    column = lax.broadcasted_iota(jnp.int32, shape, 1)
    part = column // HEAD_WIDTH
    numerator = jnp.logical_and(part == 0, row == column)
    term = (row - HEAD_WIDTH) // 3 == part - 1
    term = jnp.logical_and(term, jnp.logical_and(row >= HEAD_WIDTH, part > 0))
    return jnp.where(jnp.logical_or(numerator, term), 1.0, 0.0).astype(jnp.bfloat16)


def more_kernel(needed, sizes, packed, *refs):
    info_in, q2_ref = refs[:2]
    kv_refs = refs[2 : 2 + len(sizes)]
    acc_in, acc_ref, info_ref, kk_ref, vv_ref, key_norm, flag = refs[2 + len(sizes) :]
    z = lax.axis_index("z")
    ends = [sum(sizes[: i + 1]) for i in range(len(sizes))]
    levels = {}
    for least, end in zip(needed, ends):
        levels[least] = end
    steps = sorted(levels)

    @pl.when(pl.program_id(0) == 0)
    def _():
        key_norm[...] = jnp.zeros_like(key_norm)
        for least in steps:

            @pl.when(z >= least)
            def _(least=least):
                bounds = []
                for kv_ref, size, end, own in zip(kv_refs, sizes, ends, needed):
                    for b in range(size // BLOCK if own == least else 0):
                        part = kv_ref[b * BLOCK : (b + 1) * BLOCK, :]
                        bounds.append(stage_block(part, end - size + b * BLOCK, kk_ref, vv_ref))
                key_norm[0:1, :] = jnp.maximum(key_norm[0:1, :], functools.reduce(jnp.maximum, bounds))

        bound = jnp.where(info_in[1:2, :] > 0.5, 2.0 * SCORE_LIMIT**2, info_in[0:1, :] * key_norm[0:1, :])
        fits = jnp.max(bound) <= SCORE_LIMIT**2
        flag[0] = jnp.where(fits, 0, 1)
        put_info(info_ref, info_in[0:1, :], jnp.where(fits, 0.0, 1.0))

    def store(at, value):
        acc_ref[at : at + SUB, :] = pack(value, False) if packed else value

    @pl.when(z < steps[0])
    def _():
        for at in range(0, TILE, SUB):
            value = acc_in[at : at + SUB, :]
            acc_ref[at : at + SUB, :] = pack(value, True) if packed else value

    for index, least in enumerate(steps):
        here = z >= least
        if index + 1 < len(steps):
            here = jnp.logical_and(here, z < steps[index + 1])

        @pl.when(jnp.logical_and(here, flag[0] == 0))
        def _(least=least):
            fast_tile([levels[least]] * (TILE // SUB), q2_ref, kk_ref, vv_ref, acc_in, None, store)

    @pl.when(jnp.logical_and(z >= steps[0], flag[0] != 0))
    def _():
        blocks = jnp.int32(0)
        for least in steps:
            blocks = jnp.where(z >= least, levels[least] // BLOCK, blocks)
        value = slow_tile(blocks, q2_ref, kk_ref, vv_ref, acc_in[...])
        acc_ref[...] = pack(value, True) if packed else value


WHOLE = pl.BlockSpec(memory_space=pltpu.VMEM)


def estimate(rows, count):
    return pl.CostEstimate(
        flops=COST * 4 * rows * count * 2 * HEAD_WIDTH, bytes_accessed=rows * 2560, transcendentals=rows * count
    )


INFO = jax.ShapeDtypeStruct((8, HEAD_WIDTH), jnp.float32)


def prepare(queries):
    return pl.pallas_call(
        prepare_kernel,
        in_specs=[WHOLE] * 4,
        out_specs=[WHOLE] * 2,
        out_shape=[jax.ShapeDtypeStruct((ROWS, 256), jnp.bfloat16), INFO],
        compiler_params=pltpu.CompilerParams(vmem_limit_bytes=VMEM_LIMIT),
        cost_estimate=pl.CostEstimate(flops=ROWS * 2**15, bytes_accessed=ROWS * 768, transcendentals=0),
        name="prepare",
    )(*queries)


def attend_first(q2, info, pieces):
    count = sum(a.shape[0] for a in pieces)
    return pl.pallas_call(
        first_kernel,
        grid=(ROWS // TILE,),
        in_specs=[WHOLE, pl.BlockSpec((TILE, 256), lambda i: (i, 0))] + [WHOLE] * len(pieces),
        out_specs=[pl.BlockSpec((TILE, 256), lambda i: (i, 0)), WHOLE],
        out_shape=[jax.ShapeDtypeStruct((ROWS, 256), jnp.float32), INFO],
        scratch_shapes=[pltpu.VMEM((count, 256), jnp.bfloat16)] * 2 + [pltpu.SMEM((1,), jnp.int32)],
        compiler_params=pltpu.CompilerParams(vmem_limit_bytes=VMEM_LIMIT),
        cost_estimate=estimate(ROWS, count),
        name="attend_first",
    )(info, q2, *pieces)


def attend_more(q2, state, pieces, rows=ROWS, first_row=0, packed=False):
    acc, info = state
    pieces = sorted(pieces, key=lambda piece: piece[1])
    needed = [least for _, least in pieces]
    sizes = [a.shape[0] for a, _ in pieces]
    count = sum(sizes)
    skip = first_row // TILE
    whole = rows == ROWS
    tile_in = pl.BlockSpec((TILE, 256), lambda i: (i + skip, 0))
    return pl.pallas_call(
        functools.partial(more_kernel, tuple(needed), tuple(sizes), packed),
        grid=(rows // TILE,),
        in_specs=[WHOLE, tile_in] + [WHOLE] * len(pieces) + [tile_in],
        out_specs=[pl.BlockSpec((TILE, 256), lambda i: (i, 0)), WHOLE],
        out_shape=[jax.ShapeDtypeStruct((rows, 256), jnp.bfloat16 if packed else jnp.float32), INFO],
        scratch_shapes=[
            pltpu.VMEM((count, 256), jnp.bfloat16),
            pltpu.VMEM((count, 256), jnp.bfloat16),
            pltpu.VMEM((8, HEAD_WIDTH), jnp.float32),
            pltpu.SMEM((1,), jnp.int32),
        ],
        input_output_aliases={2 + len(pieces): 0} if whole else {},
        compiler_params=pltpu.CompilerParams(vmem_limit_bytes=VMEM_LIMIT),
        cost_estimate=estimate(rows, count),
        name="attend_more",
    )(info, q2, *[a for a, _ in pieces], acc)


def combine_kernel(acc_ref, other_ref, far_ref, own_ref, partner_ref):
    matrix = unpack_matrix()
    half = BLOCK // 2
    shape = (half, HEAD_WIDTH)
    outs = (far_ref.at[:half], far_ref.at[half:], own_ref, partner_ref)
    for part, out_ref in enumerate(outs):
        for g in range(QUERY_PER_KEY):
            at = (part * QUERY_PER_KEY + g) * half
            here = acc_ref[at : at + half, :]
            there = dot(other_ref[at : at + half, :], matrix)
            total_here = jnp.broadcast_to(here[:, TOTAL_LANE : TOTAL_LANE + 1], shape)
            total_there = there[:, HEAD_WIDTH : 2 * HEAD_WIDTH]
            shift_here = jnp.broadcast_to(here[:, SHIFT_LANE : SHIFT_LANE + 1], shape)
            shift_here = jnp.where(total_here > 0.0, shift_here, NONE)
            shift_there = jnp.where(total_there > 0.0, there[:, 2 * HEAD_WIDTH :], NONE)
            shift = jnp.maximum(shift_here, shift_there)
            scale_here = jnp.exp2(shift_here - shift)
            scale_there = jnp.exp2(shift_there - shift)
            total = total_here * scale_here + total_there * scale_there
            top = here[:, :HEAD_WIDTH] * scale_here + there[:, :HEAD_WIDTH] * scale_there
            out_ref[:, g * HEAD_WIDTH : (g + 1) * HEAD_WIDTH] = (top / total).astype(jnp.bfloat16)


def combine(acc, other):
    half, width = BLOCK // 2, QUERY_PER_KEY * HEAD_WIDTH
    return pl.pallas_call(
        combine_kernel,
        in_specs=[WHOLE] * 2,
        out_specs=[WHOLE] * 3,
        out_shape=[jax.ShapeDtypeStruct((rows, width), jnp.bfloat16) for rows in (BLOCK, half, half)],
        compiler_params=pltpu.CompilerParams(vmem_limit_bytes=VMEM_LIMIT),
        cost_estimate=pl.CostEstimate(flops=2**31, bytes_accessed=2**22, transcendentals=2**19),
        name="combine",
    )(acc, other)


def far_kernel(yh_ref, far_ref, w_ref, next_ref, previous_ref):
    half = BLOCK // 2
    result = dot(far_ref[...], w_ref[...])
    mine, partner = result[:half, :], result[half:, :]
    even = lax.axis_index("h") == 0
    next_ref[...] = jnp.where(even, mine, partner).astype(jnp.bfloat16)
    previous_ref[...] = jnp.where(even, partner, mine).astype(jnp.bfloat16)


def own_kernel(yh_ref, own_ref, partner_ref, own_w_ref, partner_w_ref, out_ref):
    out_ref[...] = dot(own_ref[...], own_w_ref[...]) + dot(partner_ref[...], partner_w_ref[...])


def project(kernel, yh, rows, weight, heads, dtype, outputs):
    width = weight.shape[1]
    cut = 512
    half = BLOCK // 2
    depth = QUERY_PER_KEY * HEAD_WIDTH

    def weight_spec(other):
        return pl.BlockSpec((depth, cut), lambda j, yh: (1 - yh[0] if other else yh[0], j))

    return pl.pallas_call(
        kernel,
        grid_spec=pltpu.PrefetchScalarGridSpec(
            num_scalar_prefetch=1,
            grid=(width // cut,),
            in_specs=[WHOLE] * len(rows) + [weight_spec(other) for other in heads],
            out_specs=[pl.BlockSpec((half, cut), lambda j, yh: (0, j))] * outputs,
        ),
        out_shape=[jax.ShapeDtypeStruct((half, width), dtype)] * outputs,
        compiler_params=pltpu.CompilerParams(vmem_limit_bytes=VMEM_LIMIT),
        cost_estimate=pl.CostEstimate(
            flops=COST * 2 * BLOCK * depth * width, bytes_accessed=depth * width * 2 * len(heads), transcendentals=0
        ),
        name="project",
    )(yh, *rows, *[weight] * len(heads))


def body(queries, key_matrix, value_matrix, out_weight):
    yh = lax.axis_index("yh")
    swap = [(0, 1), (1, 0)]
    first = yh == 0

    def pick(a, b):
        return jnp.where(first, a, b)

    def heads_of(a):
        half = a.shape[1] // 2
        return pick(a[:, :half], a[:, half:]), pick(a[:, half:], a[:, :half])

    key_mine, key_theirs = heads_of(key_matrix)
    value_mine, value_theirs = heads_of(value_matrix)
    kv_own = jnp.concatenate([key_mine, value_mine], axis=1)
    kv_theirs, kv_own, queries = lax.optimization_barrier(
        (jnp.concatenate([key_theirs, value_theirs], axis=1), kv_own, queries)
    )
    kv_partner = lax.ppermute(kv_theirs, "yh", swap)

    q_mine, q_theirs = heads_of(queries)
    q_across = lax.ppermute(q_mine, "c", swap)
    both = jnp.concatenate([kv_own, kv_partner], axis=0)
    both, q_theirs = lax.optimization_barrier((both, q_theirs))

    def around_x(a):
        moved = [lax.ppermute(a, "x", [(i, (i + s) % X_COUNT) for i in range(X_COUNT)]) for s in (1, 3, 2)]
        return moved

    near = [both] + around_x(both)

    ring = jnp.concatenate(near, axis=0)
    q_partner = lax.ppermute(q_theirs, "yh", swap)
    q_far = lax.ppermute(q_theirs, ("yh", "c"), [(i, 3 - i) for i in range(4)])
    q2, info = prepare([q_mine, q_partner, q_across, q_far])
    half = ring.shape[0] // 2
    down_pairs = [
        [(0, 7), (1, 0), (2, 1), (3, 2)],
        [(0, 7), (7, 6), (1, 0), (2, 1)],
        [(0, 7), (7, 6), (6, 5), (1, 0)],
        [(0, 7), (7, 6), (6, 5), (5, 4)],
    ]

    def around_z(up, down, s):
        down = lax.ppermute(down, "z", down_pairs[s - 1])
        return lax.ppermute(up, "z", [(i, i + 1) for i in range(s - 1, Z_COUNT - 1)]), down

    def pieces(pair, s):
        return list(zip(pair, (s, Z_COUNT - s)))

    state = attend_first(q2, info, near)
    pair = around_z(ring, ring, 1)
    for s in (1, 2, 3):
        down, up, info = lax.optimization_barrier((pair[1], pair[0], state[1]))
        state = (state[0], info)
        if s < 3:
            later = around_z(up, down, s + 1)
        else:
            later = around_z(up[:half], down[half:], s + 1)
        state = attend_more(q2, state, pieces((up, down), s))
        pair = later
    last = pieces(pair, 4)
    rows = ROWS // 2
    sent, _ = attend_more(q2, state, last, rows=rows, first_row=rows, packed=True)
    other = lax.ppermute(sent, "c", swap)
    mine, _ = attend_more(q2, state, last, rows=rows, first_row=0)
    far, near_own, near_partner = combine(mine, other)
    near_partner = lax.ppermute(near_partner, "yh", swap)
    place = yh.reshape(1).astype(jnp.int32)
    to_next, to_previous = project(far_kernel, place, [far], out_weight, [0], jnp.bfloat16, 2)

    def on_y(a, d):
        return lax.ppermute(a, ("yh", "h"), [(i, (i + d) % 4) for i in range(4)])

    parts = [on_y(to_next, 1), on_y(to_previous, 3)]
    (out,) = project(own_kernel, place, [near_own, near_partner], out_weight, [0, 1], jnp.float32, 1)
    for part in parts:
        out = out + part.astype(jnp.float32)
    return out.astype(jnp.bfloat16)


def solution(mesh):
    split = Mesh(mesh.devices.reshape(Z_COUNT, 2, X_COUNT, 2, 2), ("z", "yh", "x", "c", "h"))
    tokens = ("z", "yh", "x", "c")
    return jax.shard_map(
        body,
        mesh=split,
        in_specs=(P(tokens, "h"), P(tokens, "h"), P(tokens, "h"), P("h", None)),
        out_specs=P(tokens + ("h",), None),
        check_vma=False,
    )
```

```python
import functools
import math

import jax
import jax.numpy as jnp
from jax import lax
from jax.experimental import pallas as pl
from jax.experimental.pallas import tpu as pltpu
from jax.sharding import Mesh, PartitionSpec as P

HEAD_WIDTH = 128
QUERY_PER_KEY = 8
BLOCK = 128
ROWS = 4096
TILE = 1024
SUB = 256
LOG2_SCALE = math.log2(math.e) / math.sqrt(HEAD_WIDTH)
SCORE_LIMIT = 110.0
TOTAL_LANE = 128
SHIFT_LANE = 131
NONE = -1e30
VMEM_LIMIT = 16 * 2**20
X_COUNT, Z_COUNT = 4, 8
COST = 6


def dot_t(a, b):
    return lax.dot_general(a, b, (((1,), (1,)), ((), ())), preferred_element_type=jnp.float32)


def dot(a, b):
    return jnp.dot(a, b, preferred_element_type=jnp.float32)


def lane_iota(rows):
    return lax.broadcasted_iota(jnp.int32, (rows, 2 * HEAD_WIDTH), 1)


def squared_norms(a):
    norms = dot(a * a, jnp.full((HEAD_WIDTH, HEAD_WIDTH), 1.0, jnp.bfloat16))
    return jnp.max(norms, axis=0, keepdims=True) * 1.02


def stage_block(kv, start, kk_ref, vv_ref):
    key = kv[:, :HEAD_WIDTH]
    lane = lax.broadcasted_iota(jnp.int32, (BLOCK, HEAD_WIDTH), 1)
    rows = pl.ds(start, BLOCK)
    kk_ref[rows, :HEAD_WIDTH] = key
    kk_ref[rows, HEAD_WIDTH:] = key
    vv_ref[rows, :HEAD_WIDTH] = kv[:, HEAD_WIDTH:]
    vv_ref[rows, HEAD_WIDTH:] = jnp.where(lane < 3, 1.0, 0.0).astype(jnp.bfloat16)
    return squared_norms(key)


def key_spans(count):
    spans, at = [], 0
    while at < count:
        size = min(1024, count - at)
        spans.append((at, size))
        at += size
    return spans


def fast_tile(counts, q_ref, kk_ref, vv_ref, acc_in, mask, store):
    work = [(r, span, count) for r, count in enumerate(counts) for span in key_spans(count)]

    def scores(item):
        r, (at, size), _ = item
        return dot_t(q_ref[r * SUB : (r + 1) * SUB, :], kk_ref[at : at + size, :])

    now = scores(work[0])
    total = None
    for index, (r, (at, size), count) in enumerate(work):
        later = scores(work[index + 1]) if index + 1 < len(work) else None
        if mask is not None and at + size == count:
            now = jnp.where(mask(r * SUB, SUB, at, size), now, NONE)
        weights = jnp.exp2(now).astype(jnp.bfloat16)
        term = dot(weights, vv_ref[at : at + size, :])
        total = term if total is None else total + term
        if at + size == count:
            if acc_in is not None:
                total = acc_in[r * SUB : (r + 1) * SUB, :] + total
            store(r * SUB, total)
            total = None
        now = later


def slow_tile(blocks, q_ref, kk_ref, vv_ref, acc, mask=None):
    query = q_ref[...]

    def step(block, acc):
        at = pl.multiple_of(block * BLOCK, BLOCK)
        scores = dot_t(query, kk_ref[pl.ds(at, BLOCK), :])
        if mask is not None:
            allowed = mask(0, TILE, at, BLOCK)
            scores = jnp.where(allowed, scores, NONE)
        total = acc[:, TOTAL_LANE : TOTAL_LANE + 1]
        shift = jnp.where(total > 0.0, acc[:, SHIFT_LANE : SHIFT_LANE + 1], NONE)
        top = jnp.maximum(shift, jnp.max(scores, axis=1, keepdims=True))
        shift_now = jnp.where(top > 0.5 * NONE, top, 0.0)
        rescale = jnp.exp2(shift - shift_now)
        weights = jnp.exp2(scores - shift_now)
        if mask is not None:
            weights = jnp.where(allowed, weights, 0.0)
        weights = weights.astype(jnp.bfloat16)
        acc = acc * rescale + dot(weights, vv_ref[pl.ds(at, BLOCK), :])
        return jnp.where(lane_iota(TILE) == SHIFT_LANE, shift_now, acc)

    return lax.fori_loop(0, blocks, step, acc)


def put_info(info_ref, norm, slow):
    row = lax.broadcasted_iota(jnp.int32, (8, HEAD_WIDTH), 0)
    info_ref[...] = jnp.where(row == 0, norm, jnp.where(row == 1, slow, 0.0))


def prepare_kernel(*refs):
    q2_ref, info_ref = refs[4:]
    h = lax.axis_index("h")
    norms = []
    half = BLOCK // 2
    at = 0
    for q_refs in (refs[:2], refs[2:4]):
        for kept in (1 - h, h):
            rows = pl.ds(pl.multiple_of(kept * half, half), half)
            for q_ref in q_refs:
                for g in range(QUERY_PER_KEY):
                    wide = q_ref[rows, g * HEAD_WIDTH : (g + 1) * HEAD_WIDTH].astype(jnp.float32) * LOG2_SCALE
                    high = wide.astype(jnp.bfloat16)
                    q2_ref[at : at + half, :HEAD_WIDTH] = high
                    q2_ref[at : at + half, HEAD_WIDTH:] = (wide - high.astype(jnp.float32)).astype(jnp.bfloat16)
                    norms.append(squared_norms(high))
                    at += half
    put_info(info_ref, functools.reduce(jnp.maximum, norms) * 1.02, 0.0)


def own_mask(tile, h, yh, x, c):
    half = BLOCK // 2
    core = jnp.where(tile < 2, c, 1 - c)
    kept = jnp.where(tile % 2 == 0, 1 - h, h)

    def mask(row_at, row_count, at, size):
        shape = (row_count, size)
        row = lax.broadcasted_iota(jnp.int32, shape, 0) + row_at
        row_y = jnp.where(row < TILE // 2, yh, 1 - yh)
        token = row % half + (row_y * 8 + x * 2 + core) * BLOCK + kept * half
        lane = lax.broadcasted_iota(jnp.int32, (1, size), 1)
        key = jnp.zeros((1, size), jnp.int32)
        for b in range(size // BLOCK):
            block = at // BLOCK + b
            slot = block % X_COUNT
            back = jnp.where(slot == 1, 3, jnp.where(slot == 2, 1, jnp.where(slot == 3, 2, 0)))
            from_x = (x + back) % X_COUNT
            token_of = ((block // X_COUNT) * 8 + from_x * 2 + c) * BLOCK
            key = jnp.where(lane // BLOCK == b, token_of + lane % BLOCK, key)
        return jnp.broadcast_to(key, shape) <= token

    return mask


def first_kernel(*refs):
    info_in, q2_ref = refs[:2]
    kv_refs = refs[2 : 2 + X_COUNT]
    acc_ref, info_ref, kk_ref, vv_ref, flag = refs[2 + X_COUNT :]
    yh, x, c = lax.axis_index("yh"), lax.axis_index("x"), lax.axis_index("c")
    half = X_COUNT * BLOCK
    count = 2 * half

    @pl.when(pl.program_id(0) == 0)
    def _():
        bounds = []
        for s, kv_ref in enumerate(kv_refs):
            for partner in range(2):
                y = yh if partner == 0 else 1 - yh
                start = pl.multiple_of(y * half + s * BLOCK, BLOCK)
                bounds.append(stage_block(kv_ref[partner * BLOCK : (partner + 1) * BLOCK, :], start, kk_ref, vv_ref))
        fits = jnp.max(functools.reduce(jnp.maximum, bounds) * info_in[0:1, :]) <= SCORE_LIMIT**2
        flag[0] = jnp.where(fits, 0, 1)
        put_info(info_ref, info_in[0:1, :], jnp.where(fits, 0.0, 1.0))

    mask = own_mask(pl.program_id(0), lax.axis_index("h"), yh, x, c)

    def store(at, value):
        acc_ref[at : at + SUB, :] = value

    subs = TILE // SUB // 2
    for y in range(2):

        @pl.when(jnp.logical_and(flag[0] == 0, yh == y))
        def _(y=y):
            counts = [half * (1 + y)] * subs + [half * (2 - y)] * subs
            fast_tile(counts, q2_ref, kk_ref, vv_ref, None, mask, store)

    @pl.when(flag[0] != 0)
    def _():
        acc = jnp.zeros((TILE, 2 * HEAD_WIDTH), jnp.float32)
        acc_ref[...] = slow_tile(count // BLOCK, q2_ref, kk_ref, vv_ref, acc, mask)


def pack(acc, shifted):
    shape = (acc.shape[0], HEAD_WIDTH)
    lane = lax.broadcasted_iota(jnp.int32, shape, 1)
    left = acc[:, HEAD_WIDTH:]
    if shifted:
        shift = jnp.broadcast_to(acc[:, SHIFT_LANE : SHIFT_LANE + 1], shape)
        left = jnp.where(jnp.logical_and(lane >= 3, lane < 6), shift, left)
    right = jnp.zeros(shape, jnp.float32)
    for t in range(3):
        term = left.astype(jnp.bfloat16).astype(jnp.float32)
        right = jnp.where(jnp.logical_or(lane == t, lane == 3 + t), term, right)
        left = left - term
    return jnp.concatenate([acc[:, :HEAD_WIDTH].astype(jnp.bfloat16), right.astype(jnp.bfloat16)], axis=1)


def unpack_matrix():
    shape = (2 * HEAD_WIDTH, 3 * HEAD_WIDTH)
    row = lax.broadcasted_iota(jnp.int32, shape, 0)
    column = lax.broadcasted_iota(jnp.int32, shape, 1)
    part = column // HEAD_WIDTH
    numerator = jnp.logical_and(part == 0, row == column)
    term = (row - HEAD_WIDTH) // 3 == part - 1
    term = jnp.logical_and(term, jnp.logical_and(row >= HEAD_WIDTH, part > 0))
    return jnp.where(jnp.logical_or(numerator, term), 1.0, 0.0).astype(jnp.bfloat16)


def more_kernel(needed, sizes, packed, *refs):
    info_in, q2_ref = refs[:2]
    kv_refs = refs[2 : 2 + len(sizes)]
    acc_in, acc_ref, info_ref, kk_ref, vv_ref, key_norm, flag = refs[2 + len(sizes) :]
    z = lax.axis_index("z")
    ends = [sum(sizes[: i + 1]) for i in range(len(sizes))]
    levels = {}
    for least, end in zip(needed, ends):
        levels[least] = end
    steps = sorted(levels)

    @pl.when(pl.program_id(0) == 0)
    def _():
        key_norm[...] = jnp.zeros_like(key_norm)
        for least in steps:

            @pl.when(z >= least)
            def _(least=least):
                bounds = []
                for kv_ref, size, end, own in zip(kv_refs, sizes, ends, needed):
                    for b in range(size // BLOCK if own == least else 0):
                        part = kv_ref[b * BLOCK : (b + 1) * BLOCK, :]
                        bounds.append(stage_block(part, end - size + b * BLOCK, kk_ref, vv_ref))
                key_norm[0:1, :] = jnp.maximum(key_norm[0:1, :], functools.reduce(jnp.maximum, bounds))

        bound = jnp.where(info_in[1:2, :] > 0.5, 2.0 * SCORE_LIMIT**2, info_in[0:1, :] * key_norm[0:1, :])
        fits = jnp.max(bound) <= SCORE_LIMIT**2
        flag[0] = jnp.where(fits, 0, 1)
        put_info(info_ref, info_in[0:1, :], jnp.where(fits, 0.0, 1.0))

    def store(at, value):
        acc_ref[at : at + SUB, :] = pack(value, False) if packed else value

    @pl.when(z < steps[0])
    def _():
        for at in range(0, TILE, SUB):
            value = acc_in[at : at + SUB, :]
            acc_ref[at : at + SUB, :] = pack(value, True) if packed else value

    for index, least in enumerate(steps):
        here = z >= least
        if index + 1 < len(steps):
            here = jnp.logical_and(here, z < steps[index + 1])

        @pl.when(jnp.logical_and(here, flag[0] == 0))
        def _(least=least):
            fast_tile([levels[least]] * (TILE // SUB), q2_ref, kk_ref, vv_ref, acc_in, None, store)

    @pl.when(jnp.logical_and(z >= steps[0], flag[0] != 0))
    def _():
        blocks = jnp.int32(0)
        for least in steps:
            blocks = jnp.where(z >= least, levels[least] // BLOCK, blocks)
        value = slow_tile(blocks, q2_ref, kk_ref, vv_ref, acc_in[...])
        acc_ref[...] = pack(value, True) if packed else value


WHOLE = pl.BlockSpec(memory_space=pltpu.VMEM)


def estimate(rows, count):
    return pl.CostEstimate(
        flops=COST * 4 * rows * count * 2 * HEAD_WIDTH, bytes_accessed=rows * 2560, transcendentals=rows * count
    )


INFO = jax.ShapeDtypeStruct((8, HEAD_WIDTH), jnp.float32)


def prepare(queries):
    return pl.pallas_call(
        prepare_kernel,
        in_specs=[WHOLE] * 4,
        out_specs=[WHOLE] * 2,
        out_shape=[jax.ShapeDtypeStruct((ROWS, 256), jnp.bfloat16), INFO],
        compiler_params=pltpu.CompilerParams(vmem_limit_bytes=VMEM_LIMIT),
        cost_estimate=pl.CostEstimate(flops=ROWS * 2**15, bytes_accessed=ROWS * 768, transcendentals=0),
        name="prepare",
    )(*queries)


def attend_first(q2, info, pieces):
    count = sum(a.shape[0] for a in pieces)
    return pl.pallas_call(
        first_kernel,
        grid=(ROWS // TILE,),
        in_specs=[WHOLE, pl.BlockSpec((TILE, 256), lambda i: (i, 0))] + [WHOLE] * len(pieces),
        out_specs=[pl.BlockSpec((TILE, 256), lambda i: (i, 0)), WHOLE],
        out_shape=[jax.ShapeDtypeStruct((ROWS, 256), jnp.float32), INFO],
        scratch_shapes=[pltpu.VMEM((count, 256), jnp.bfloat16)] * 2 + [pltpu.SMEM((1,), jnp.int32)],
        compiler_params=pltpu.CompilerParams(vmem_limit_bytes=VMEM_LIMIT),
        cost_estimate=estimate(ROWS, count),
        name="attend_first",
    )(info, q2, *pieces)


def attend_more(q2, state, pieces, rows=ROWS, first_row=0, packed=False):
    acc, info = state
    pieces = sorted(pieces, key=lambda piece: piece[1])
    needed = [least for _, least in pieces]
    sizes = [a.shape[0] for a, _ in pieces]
    count = sum(sizes)
    skip = first_row // TILE
    whole = rows == ROWS
    tile_in = pl.BlockSpec((TILE, 256), lambda i: (i + skip, 0))
    return pl.pallas_call(
        functools.partial(more_kernel, tuple(needed), tuple(sizes), packed),
        grid=(rows // TILE,),
        in_specs=[WHOLE, tile_in] + [WHOLE] * len(pieces) + [tile_in],
        out_specs=[pl.BlockSpec((TILE, 256), lambda i: (i, 0)), WHOLE],
        out_shape=[jax.ShapeDtypeStruct((rows, 256), jnp.bfloat16 if packed else jnp.float32), INFO],
        scratch_shapes=[
            pltpu.VMEM((count, 256), jnp.bfloat16),
            pltpu.VMEM((count, 256), jnp.bfloat16),
            pltpu.VMEM((8, HEAD_WIDTH), jnp.float32),
            pltpu.SMEM((1,), jnp.int32),
        ],
        input_output_aliases={2 + len(pieces): 0} if whole else {},
        compiler_params=pltpu.CompilerParams(vmem_limit_bytes=VMEM_LIMIT),
        cost_estimate=estimate(rows, count),
        name="attend_more",
    )(info, q2, *[a for a, _ in pieces], acc)


def combine_kernel(acc_ref, other_ref, far_ref, own_ref, partner_ref):
    matrix = unpack_matrix()
    half = BLOCK // 2
    shape = (half, HEAD_WIDTH)
    outs = (far_ref.at[:half], far_ref.at[half:], own_ref, partner_ref)
    for part, out_ref in enumerate(outs):
        for g in range(QUERY_PER_KEY):
            at = (part * QUERY_PER_KEY + g) * half
            here = acc_ref[at : at + half, :]
            there = dot(other_ref[at : at + half, :], matrix)
            total_here = jnp.broadcast_to(here[:, TOTAL_LANE : TOTAL_LANE + 1], shape)
            total_there = there[:, HEAD_WIDTH : 2 * HEAD_WIDTH]
            shift_here = jnp.broadcast_to(here[:, SHIFT_LANE : SHIFT_LANE + 1], shape)
            shift_here = jnp.where(total_here > 0.0, shift_here, NONE)
            shift_there = jnp.where(total_there > 0.0, there[:, 2 * HEAD_WIDTH :], NONE)
            shift = jnp.maximum(shift_here, shift_there)
            scale_here = jnp.exp2(shift_here - shift)
            scale_there = jnp.exp2(shift_there - shift)
            total = total_here * scale_here + total_there * scale_there
            top = here[:, :HEAD_WIDTH] * scale_here + there[:, :HEAD_WIDTH] * scale_there
            out_ref[:, g * HEAD_WIDTH : (g + 1) * HEAD_WIDTH] = (top / total).astype(jnp.bfloat16)


def combine(acc, other):
    half, width = BLOCK // 2, QUERY_PER_KEY * HEAD_WIDTH
    return pl.pallas_call(
        combine_kernel,
        in_specs=[WHOLE] * 2,
        out_specs=[WHOLE] * 3,
        out_shape=[jax.ShapeDtypeStruct((rows, width), jnp.bfloat16) for rows in (BLOCK, half, half)],
        compiler_params=pltpu.CompilerParams(vmem_limit_bytes=VMEM_LIMIT),
        cost_estimate=pl.CostEstimate(flops=2**31, bytes_accessed=2**22, transcendentals=2**19),
        name="combine",
    )(acc, other)


def far_kernel(yh_ref, far_ref, w_ref, next_ref, previous_ref):
    half = BLOCK // 2
    result = dot(far_ref[...], w_ref[...])
    mine, partner = result[:half, :], result[half:, :]
    even = lax.axis_index("h") == 0
    next_ref[...] = jnp.where(even, mine, partner).astype(jnp.bfloat16)
    previous_ref[...] = jnp.where(even, partner, mine).astype(jnp.bfloat16)


def own_kernel(yh_ref, own_ref, partner_ref, own_w_ref, partner_w_ref, out_ref):
    out_ref[...] = dot(own_ref[...], own_w_ref[...]) + dot(partner_ref[...], partner_w_ref[...])


def project(kernel, yh, rows, weight, heads, dtype, outputs):
    width = weight.shape[1]
    cut = 512
    half = BLOCK // 2
    depth = QUERY_PER_KEY * HEAD_WIDTH

    def weight_spec(other):
        return pl.BlockSpec((depth, cut), lambda j, yh: (1 - yh[0] if other else yh[0], j))

    return pl.pallas_call(
        kernel,
        grid_spec=pltpu.PrefetchScalarGridSpec(
            num_scalar_prefetch=1,
            grid=(width // cut,),
            in_specs=[WHOLE] * len(rows) + [weight_spec(other) for other in heads],
            out_specs=[pl.BlockSpec((half, cut), lambda j, yh: (0, j))] * outputs,
        ),
        out_shape=[jax.ShapeDtypeStruct((half, width), dtype)] * outputs,
        compiler_params=pltpu.CompilerParams(vmem_limit_bytes=VMEM_LIMIT),
        cost_estimate=pl.CostEstimate(
            flops=COST * 2 * BLOCK * depth * width, bytes_accessed=depth * width * 2 * len(heads), transcendentals=0
        ),
        name="project",
    )(yh, *rows, *[weight] * len(heads))


def body(queries, key_matrix, value_matrix, out_weight):
    yh = lax.axis_index("yh")
    swap = [(0, 1), (1, 0)]
    first = yh == 0

    def pick(a, b):
        return jnp.where(first, a, b)

    def heads_of(a):
        half = a.shape[1] // 2
        return pick(a[:, :half], a[:, half:]), pick(a[:, half:], a[:, :half])

    key_mine, key_theirs = heads_of(key_matrix)
    value_mine, value_theirs = heads_of(value_matrix)
    kv_own = jnp.concatenate([key_mine, value_mine], axis=1)
    kv_theirs, kv_own, queries = lax.optimization_barrier(
        (jnp.concatenate([key_theirs, value_theirs], axis=1), kv_own, queries)
    )
    kv_partner = lax.ppermute(kv_theirs, "yh", swap)

    q_mine, q_theirs = heads_of(queries)
    both = jnp.concatenate([kv_own, kv_partner], axis=0)
    both, q_theirs = lax.optimization_barrier((both, q_theirs))

    def around_x(a):
        moved = [lax.ppermute(a, "x", [(i, (i + s) % X_COUNT) for i in range(X_COUNT)]) for s in (1, 3, 2)]
        return moved

    near = [both] + around_x(both)
    fourth = lax.ppermute(both, "z", [(i, i + 4) for i in range(Z_COUNT - 4)])

    ring = jnp.concatenate(near, axis=0)
    q_partner = lax.ppermute(q_theirs, "yh", swap)
    q_far = lax.ppermute(q_theirs, ("yh", "c"), [(i, 3 - i) for i in range(4)])
    q_mine, q_partner = lax.optimization_barrier((q_mine, q_partner))
    q_across = lax.ppermute(q_mine, "c", swap)
    q2, info = prepare([q_mine, q_partner, q_across, q_far])
    down_pairs = [[(0, 7), (1, 0), (2, 1)], [(0, 7), (7, 6), (1, 0)], [(0, 7), (7, 6), (6, 5)]]

    def around_z(up, down, s):
        down = lax.ppermute(down, "z", down_pairs[s - 1])
        return lax.ppermute(up, "z", [(i, i + 1) for i in range(s - 1, Z_COUNT - 1)]), down

    def pieces(pair, s):
        return list(zip(pair, (s, Z_COUNT - s)))

    def after(pair, state):
        down, up, info = lax.optimization_barrier((pair[1], pair[0], state[1]))
        return (up, down), (state[0], info)

    state = attend_first(q2, info, near)
    pair = around_z(ring, ring, 1)
    fourth, info = lax.optimization_barrier((fourth, state[1]))
    fourths = [(a, 4) for a in around_x(fourth)]
    pair, state = after(pair, (state[0], info))
    later = around_z(*pair, 2)
    state = attend_more(q2, state, pieces(pair, 1) + [(fourth, 4)])
    pair, state = after(later, state)
    later = around_z(*pair, 3)
    state = attend_more(q2, state, pieces(pair, 2) + fourths)
    pair, state = after(later, state)
    rows = ROWS // 2
    last = pieces(pair, 3)
    sent, _ = attend_more(q2, state, last, rows=rows, first_row=rows, packed=True)
    other = lax.ppermute(sent, "c", swap)
    mine, _ = attend_more(q2, state, last, rows=rows, first_row=0)
    far, near_own, near_partner = combine(mine, other)
    near_partner = lax.ppermute(near_partner, "yh", swap)
    place = yh.reshape(1).astype(jnp.int32)
    to_next, to_previous = project(far_kernel, place, [far], out_weight, [0], jnp.bfloat16, 2)

    def on_y(a, d):
        return lax.ppermute(a, ("yh", "h"), [(i, (i + d) % 4) for i in range(4)])

    parts = [on_y(to_next, 1), on_y(to_previous, 3)]
    (out,) = project(own_kernel, place, [near_own, near_partner], out_weight, [0, 1], jnp.float32, 1)
    for part in parts:
        out = out + part.astype(jnp.float32)
    return out.astype(jnp.bfloat16)


def solution(mesh):
    split = Mesh(mesh.devices.reshape(Z_COUNT, 2, X_COUNT, 2, 2), ("z", "yh", "x", "c", "h"))
    tokens = ("z", "yh", "x", "c")
    return jax.shard_map(
        body,
        mesh=split,
        in_specs=(P(tokens, "h"), P(tokens, "h"), P(tokens, "h"), P("h", None)),
        out_specs=P(tokens + ("h",), None),
        check_vma=False,
    )
```
